32 devices in a mesh: groups: 2 (over y), lat: 8 (over z, core), row: 2 (over x).
Axes of the slice: x: 2, y: 2, z: 4, core: 2. Of those that a mesh axis runs over, the one named last changes fastest.
Arguments:
- stream_rows: bfloat16 [2048, 4096], P(('groups', 'lat'), 'row'), parts along dimension 0, may hold values from -6 to 6
- active_blocks: int32 [2048, 3], P(('groups', 'lat')), parts along dimension 0, may hold values from 0 to 7, all different within a row; in each aligned block of 128 rows (0 to 127, 128 to 255, ...) at most 96 rows name the same one
- encoder_weight: bfloat16 [8192, 1024], P(('groups', 'row'), 'lat'), parts along dimension 0, may hold values from -0.09375 to 0.09375
- encoder_bias: float32 [2048], P(('groups', 'lat')), parts along dimension 0, may hold values from -3 to 3
- decoder_weight: bfloat16 [2048, 4096], P(('groups', 'lat'), 'row'), parts along dimension 0, may hold values from -0.3125 to 0.3125
- decoder_bias: float32 [8192], P(('groups', 'row')), parts along dimension 0, may hold values from -3 to 3
- encoder_first: bfloat16 [8192, 1024], P(('groups', 'row'), 'lat'), parts along dimension 0, may hold values from -2 to 2
- encoder_second: bfloat16 [8192, 1024], P(('groups', 'row'), 'lat'), parts along dimension 0, may hold values from 0.0099487305 to 1
- decoder_first: bfloat16 [2048, 4096], P(('groups', 'lat'), 'row'), parts along dimension 0, may hold values from -2 to 2
- decoder_second: bfloat16 [2048, 4096], P(('groups', 'lat'), 'row'), parts along dimension 0, may hold values from 0.0099487305 to 1
Outputs:
- encoder_next: bfloat16 [8192, 1024], P(('groups', 'row'), 'lat'), parts along dimension 0
- encoder_first_next: bfloat16 [8192, 1024], P(('groups', 'row'), 'lat'), parts along dimension 0
- encoder_second_next: bfloat16 [8192, 1024], P(('groups', 'row'), 'lat'), parts along dimension 0
- decoder_next: bfloat16 [2048, 4096], P(('groups', 'lat'), 'row'), parts along dimension 0
- decoder_first_next: bfloat16 [2048, 4096], P(('groups', 'lat'), 'row'), parts along dimension 0
- decoder_second_next: bfloat16 [2048, 4096], P(('groups', 'lat'), 'row'), parts along dimension 0
- encoder_bias_grad: float32 [2048], P(('groups', 'lat')), parts along dimension 0
- decoder_bias_grad: float32 [8192], P(('groups', 'row')), parts along dimension 0
The draws below stay inside these ranges and needn't reach their ends.
There are 2 independent parts, one for each index of `groups`. The reference program is written for one: setup_inputs(seed, part) draws one part's arguments, and reference() takes and returns one part's arrays. A program takes and returns all parts, laid end to end along the dimension named above; each array names one. Nothing has to cross between parts.
Inputs may be any that keep to these rules, and one draw needn't show every extreme that they name: `active_blocks`: each row names 3 different latent blocks. In every aligned block of 128 rows (the rows of one index of lat) no latent block is named by more than 96 rows, and some latent block is named by exactly 96 of them. Every latent block is named by some row.
All inputs are finite; a program needn't handle non-finite values.
Results may differ from the reference program's by a relative error of at most 0.0056.
Values may be sent and summed in bfloat16 or wider, within the bound.
A program may use at most 64 MiB of HBM per device.

```python
import math
import jax
import jax.numpy as jnp
import numpy as np
from jax import lax

D = 4096
BLOCK = 128
KB = 3
ROW_DEV = 128
ROWS = 1024
LATENTS = 1024
CAP = 96
N_LAT = 8


def block_scale(rng, dims, pieces, low, high):
    loudness = 1.0
    for axis_at, blocks in pieces:
        heights = jax.random.uniform(jax.random.fold_in(jax.random.fold_in(rng, 6), axis_at), (blocks,), jnp.float32, low / len(pieces), high / len(pieces))
        loudness = loudness * jnp.repeat(jnp.exp(heights), dims[axis_at] // blocks).reshape((-1,) + (1,) * (len(dims) - 1 - axis_at))
    return loudness


def shared_out(own_key, own, number, rows, number_of, top, reach, lean):
    order = jax.random.permutation(own_key, number_of)
    heavy_load, usual = portions_of(number_of, rows * top, reach, lean, True), portions_of(number_of, rows * top, reach, lean, False)
    places = jnp.arange(number_of)

    def named(lengths, turn):
        used = int((lengths > 0).sum())
        fixed = max(1, used // 4)
        shifted = fixed + (places - fixed + turn * (used - fixed)) % max(1, number_of - fixed)
        return jnp.zeros((number_of,), jnp.int32).at[order[jnp.where(places < fixed, places, shifted)]].set(jnp.asarray(lengths, jnp.int32))

    lengths = jnp.where(number % 4 == 0, named(heavy_load, number // 4), named(usual, number - number // 4 - 1))
    mixed = jax.random.permutation(jax.random.fold_in(own, 3), number_of)
    giver, sink = mixed[0:number_of // 2 * 2:2], mixed[1:number_of // 2 * 2:2]
    room = jnp.minimum(lengths[giver] - 1, reach - lengths[sink]) // 2
    room = jnp.where((giver == order[0]) | (sink == order[0]) | (lengths[sink] == 0), 0, jnp.maximum(room, 0))
    shifted = jax.random.randint(jax.random.fold_in(own, 4), (number_of // 2,), 0, 1 << 20) % (room + 1)
    lengths = lengths.at[giver].add(-shifted).at[sink].add(shifted)
    members = jnp.searchsorted(jnp.cumsum(lengths), jnp.arange(rows * top), side="right").astype(jnp.int32)
    listing = members.reshape(top, rows).T
    listing = listing[jax.random.permutation(jax.random.fold_in(own, 1), rows)]
    turn = jax.random.randint(jax.random.fold_in(own, 2), (rows, 1), 0, top)
    return jnp.take_along_axis(listing, (jnp.arange(top)[None, :] + turn) % top, axis=1)


def portions_of(count, total, reach, lean, full):
    portions = [(1 << 20) // math.isqrt(grade ** lean) + 1 for grade in range(1, count + 1)]
    largest = reach if full else min(reach, max(-(-total // count), total * portions[0] // sum(portions)))
    least = 1 if total - largest >= count - 1 else 0
    holding, rest = [largest] + [least] * (count - 1), total - largest - least * (count - 1)
    while rest > 0:
        candidates = [i for i in range(1, count) if holding[i] < largest] or [i for i in range(1, count) if holding[i] < reach]
        whole, left = sum([portions[i] for i in candidates]), rest
        for i in candidates:
            extra = min(reach - holding[i], max(1, left * portions[i] // whole), rest)
            holding[i] = holding[i] + extra
            rest = rest - extra
    return np.array(holding)


def normal_values(stream_key, dims, width, bound, split=(), kind=jnp.bfloat16):
    array = jax.random.normal(stream_key, dims, jnp.float32) * width
    if len(split) > 0:
        array = block_scale(stream_key, dims, split, -0.22, 0.18) * array
    return jnp.clip(array, min=-bound, max=bound).astype(kind)


def setup_inputs(seed: int = 0, part: int = 0) -> dict:
    key_of = jax.random.split(jax.random.key(seed), 11)
    part_keys = jax.random.split(jax.random.fold_in(key_of[10], part), 11)
    stream_rows = normal_values(part_keys[0], (ROWS, D), 1.0, 6.0, ((0, 8), (1, 2)))
    active_blocks_keys = jax.random.split(jax.random.fold_in(part_keys[1], 1), ROWS // ROW_DEV)
    active_blocks_turns = jax.random.permutation(jax.random.fold_in(part_keys[1], 3), ROWS // ROW_DEV)
    active_blocks = jax.vmap(lambda own, number: shared_out(jax.random.fold_in(part_keys[1], 2), own, number, ROW_DEV, N_LAT, KB, CAP, 2))(active_blocks_keys, active_blocks_turns).reshape((ROWS, KB))
    encoder_weight = normal_values(part_keys[2], (D, LATENTS), D ** -0.5, 0.09375, ((0, 2), (1, 8)))
    encoder_bias = normal_values(part_keys[3], (LATENTS,), 0.5, 3.0, ((0, 8),), jnp.float32)
    decoder_weight = normal_values(part_keys[4], (LATENTS, D), (KB * BLOCK) ** -0.5, 0.3125, ((0, 8), (1, 2)))
    decoder_bias = normal_values(part_keys[5], (D,), 0.5, 3.0, ((0, 2),), jnp.float32)
    encoder_first = normal_values(part_keys[6], (D, LATENTS), 0.3, 2.0, ((0, 2), (1, 8)))
    encoder_second = jnp.clip(jnp.exp(math.log(1.0) - 4.61031033 * jax.random.uniform(part_keys[7], (D, LATENTS), jnp.float32) ** block_scale(part_keys[7], (D, LATENTS), ((0, 2), (1, 8)), -0.2, 0.2)), 0.0099487305, 1.0).astype(jnp.bfloat16)
    decoder_first = normal_values(part_keys[8], (LATENTS, D), 0.3, 2.0, ((0, 8), (1, 2)))
    decoder_second = jnp.clip(jnp.exp(math.log(1.0) - 4.61031033 * jax.random.uniform(part_keys[9], (LATENTS, D), jnp.float32) ** block_scale(part_keys[9], (LATENTS, D), ((0, 8), (1, 2)), -0.2, 0.2)), 0.0099487305, 1.0).astype(jnp.bfloat16)
    return {"stream_rows": stream_rows, "active_blocks": active_blocks, "encoder_weight": encoder_weight, "encoder_bias": encoder_bias, "decoder_weight": decoder_weight, "decoder_bias": decoder_bias, "encoder_first": encoder_first, "encoder_second": encoder_second, "decoder_first": decoder_first, "decoder_second": decoder_second}


beta_one = 0.9
beta_two = 0.999
step_rate = 0.01
epsilon = 1e-08

def slot_tables(active_blocks):
    chosen = active_blocks.reshape(N_LAT, ROW_DEV * KB)
    one_hot = (chosen[:, :, None] == jnp.arange(N_LAT, dtype=jnp.int32)[None, None, :]).astype(jnp.int32)
    position = lax.optimization_barrier(jnp.sum((jnp.cumsum(one_hot, axis=1) - 1) * one_hot, axis=2)).astype(jnp.int32)
    source = jnp.broadcast_to(jnp.arange(N_LAT, dtype=jnp.int32)[:, None], chosen.shape)
    entry_pos = jnp.broadcast_to(jnp.arange(ROW_DEV * KB, dtype=jnp.int32)[None, :], chosen.shape)
    row_index = (source * ROW_DEV + entry_pos // KB).astype(jnp.int32)
    slot_table = jnp.zeros((N_LAT, N_LAT, CAP), jnp.int32).at[chosen, source, position].set(row_index)
    slot_live = jnp.zeros((N_LAT, N_LAT, CAP), jnp.float32).at[chosen, source, position].set(1.0)
    return (slot_table.reshape(N_LAT, N_LAT * CAP), slot_live.reshape(N_LAT, N_LAT * CAP))

def adam_update(weight, moment_one, moment_two, gradient):
    first_next = beta_one * moment_one.astype(jnp.float32) + (1.0 - beta_one) * gradient
    second_next = beta_two * moment_two.astype(jnp.float32) + (1.0 - beta_two) * gradient * gradient
    weight_next = weight.astype(jnp.float32) - step_rate * first_next / (jnp.sqrt(second_next) + epsilon)
    return (weight_next.astype(jnp.bfloat16), first_next.astype(jnp.bfloat16), second_next.astype(jnp.bfloat16))

def encode_block(stream_rows, row_index, live_col, in_weight, in_bias):
    routed_rows = stream_rows[row_index] * live_col.astype(jnp.bfloat16)
    preact = jnp.dot(routed_rows, in_weight, preferred_element_type=jnp.float32) + in_bias
    code_vals = jax.nn.softplus(preact).astype(jnp.bfloat16)
    return (routed_rows, preact, code_vals)

def reference(stream_rows, active_blocks, encoder_weight, encoder_bias, decoder_weight, decoder_bias, encoder_first, encoder_second, decoder_first, decoder_second):
    slot_table, slot_live = slot_tables(active_blocks)
    enc_blocks = encoder_weight.reshape(D, N_LAT, BLOCK).transpose(1, 0, 2)
    dec_blocks = decoder_weight.reshape(N_LAT, BLOCK, D)
    bias_blocks = encoder_bias.reshape(N_LAT, BLOCK)
    block_inputs = (slot_table, slot_live, enc_blocks, bias_blocks, dec_blocks)

    def forward_pass(rebuilt, inputs_here):
        row_index, live_row, in_weight, in_bias, out_weight = inputs_here
        live_col = live_row[:, None]
        routed_rows, preact, code_vals = encode_block(stream_rows, row_index, live_col, in_weight, in_bias)
        portion = jnp.dot(code_vals, out_weight, preferred_element_type=jnp.float32).astype(jnp.bfloat16)
        rebuilt = rebuilt.at[row_index].add(portion.astype(jnp.float32) * live_col)
        return (rebuilt, None)
    rebuilt, unused = lax.scan(forward_pass, jnp.zeros((ROWS, D), jnp.float32), block_inputs)
    rebuilt = rebuilt + decoder_bias
    residual = rebuilt - stream_rows.astype(jnp.float32)
    loss_scale = 1.0 / math.sqrt(KB * ROW_DEV)
    decoder_bias_grad = loss_scale * lax.optimization_barrier(jnp.sum(residual, axis=0))
    error_rows = (residual * loss_scale).astype(jnp.bfloat16)

    def backward_pass(state_carry, inputs_here):
        row_index, live_row, in_weight, in_bias, out_weight = inputs_here
        live_col = live_row[:, None]
        routed_rows, preact, code_vals = encode_block(stream_rows, row_index, live_col, in_weight, in_bias)
        routed_error = error_rows[row_index] * live_col.astype(jnp.bfloat16)
        code_grad = lax.dot_general(routed_error, out_weight, (((1,), (1,)), ((), ())), preferred_element_type=jnp.float32)
        preact_grad = code_grad * jax.nn.sigmoid(preact)
        bias_grad = lax.optimization_barrier(jnp.sum(preact_grad, axis=0))
        preact_low = preact_grad.astype(jnp.bfloat16)
        in_grad = lax.dot_general(routed_rows, preact_low, (((0,), (0,)), ((), ())), preferred_element_type=jnp.float32)
        out_grad = lax.dot_general(code_vals, routed_error, (((0,), (0,)), ((), ())), preferred_element_type=jnp.float32)
        return (state_carry, (in_grad, out_grad, bias_grad))
    unused, grads = lax.scan(backward_pass, jnp.zeros((), jnp.float32), block_inputs)
    in_grads, out_grads, bias_grads = grads
    encoder_grad = in_grads.transpose(1, 0, 2).reshape(D, LATENTS)
    decoder_grad = out_grads.reshape(LATENTS, D)
    encoder_bias_grad = bias_grads.reshape(LATENTS)
    encoder_next, encoder_first_next, encoder_second_next = adam_update(encoder_weight, encoder_first, encoder_second, encoder_grad)
    decoder_next, decoder_first_next, decoder_second_next = adam_update(decoder_weight, decoder_first, decoder_second, decoder_grad)
    return (encoder_next, encoder_first_next, encoder_second_next, decoder_next, decoder_first_next, decoder_second_next, encoder_bias_grad, decoder_bias_grad)
```

```python
import math

import jax
import jax.numpy as jnp
from jax import lax
from jax.sharding import PartitionSpec as P

beta_one = 0.9
beta_two = 0.999
step_rate = 0.01
epsilon = 1e-08


def adam_update(weight, moment_one, moment_two, gradient):
    first_next = beta_one * moment_one.astype(jnp.float32) + (1.0 - beta_one) * gradient
    second_next = beta_two * moment_two.astype(jnp.float32) + (1.0 - beta_two) * gradient * gradient
    weight_next = weight.astype(jnp.float32) - step_rate * first_next / (
        jnp.sqrt(second_next) + epsilon
    )
    return (
        weight_next.astype(jnp.bfloat16),
        first_next.astype(jnp.bfloat16),
        second_next.astype(jnp.bfloat16),
    )


def contract_rows(left, right):
    return lax.dot_general(
        left, right, (((0,), (0,)), ((), ())), preferred_element_type=jnp.float32
    )


def contract_cols(left, right):
    return lax.dot_general(
        left, right, (((1,), (1,)), ((), ())), preferred_element_type=jnp.float32
    )


def routed_step(
    stream_rows,
    active_blocks,
    encoder_weight,
    encoder_bias,
    decoder_weight,
    decoder_bias,
    encoder_first,
    encoder_second,
    decoder_first,
    decoder_second,
):
    lat_count = lax.axis_size("lat")
    row_count = stream_rows.shape[0]
    width_part = stream_rows.shape[1]
    picks = active_blocks.shape[1]
    capacity = min(row_count, 2 * row_count * picks // lat_count)
    slot_total = lat_count * capacity
    loss_scale = 1.0 / math.sqrt(picks * row_count)
    chosen = active_blocks.reshape(-1)
    one_hot = (chosen[:, None] == jnp.arange(lat_count, dtype=jnp.int32)[None, :]).astype(jnp.int32)
    position = jnp.sum((jnp.cumsum(one_hot, axis=0) - 1) * one_hot, axis=1)
    slot_index = chosen * capacity + position
    owner_row = jnp.arange(chosen.shape[0], dtype=jnp.int32) // picks
    slot_row = jnp.zeros((slot_total,), jnp.int32).at[slot_index].set(owner_row)
    slot_live = jnp.zeros((slot_total,), jnp.bfloat16).at[slot_index].set(1.0)
    outgoing = (stream_rows[slot_row] * slot_live[:, None]).reshape(lat_count, capacity, width_part)
    routed_rows = lax.all_to_all(outgoing, "lat", split_axis=0, concat_axis=0, tiled=True).reshape(
        slot_total, width_part
    )
    preact_part = jnp.dot(routed_rows, encoder_weight, preferred_element_type=jnp.float32)
    preact = lax.psum(preact_part, "row") + encoder_bias
    code_vals = jax.nn.softplus(preact).astype(jnp.bfloat16)
    portion = jnp.dot(code_vals, decoder_weight, preferred_element_type=jnp.float32).astype(
        jnp.bfloat16
    )
    returned = lax.all_to_all(
        portion.reshape(lat_count, capacity, width_part),
        "lat",
        split_axis=0,
        concat_axis=0,
        tiled=True,
    )
    picked = returned.reshape(slot_total, width_part)[slot_index].reshape(
        row_count, picks, width_part
    )
    rebuilt = jnp.sum(picked.astype(jnp.float32), axis=1) + decoder_bias
    residual = rebuilt - stream_rows.astype(jnp.float32)
    decoder_bias_grad = lax.psum(loss_scale * jnp.sum(residual, axis=0), "lat")
    error_local = (residual * loss_scale).astype(jnp.bfloat16)
    outgoing_error = (error_local[slot_row] * slot_live[:, None]).reshape(
        lat_count, capacity, width_part
    )
    routed_error = lax.all_to_all(
        outgoing_error, "lat", split_axis=0, concat_axis=0, tiled=True
    ).reshape(slot_total, width_part)
    code_part = contract_cols(routed_error, decoder_weight)
    code_grad = lax.psum(code_part, "row")
    preact_grad = code_grad * jax.nn.sigmoid(preact)
    encoder_bias_grad = jnp.sum(preact_grad, axis=0)
    preact_low = preact_grad.astype(jnp.bfloat16)
    encoder_grad = contract_rows(routed_rows, preact_low)
    decoder_grad = contract_rows(code_vals, routed_error)
    encoder_next, encoder_first_next, encoder_second_next = adam_update(
        encoder_weight, encoder_first, encoder_second, encoder_grad
    )
    decoder_next, decoder_first_next, decoder_second_next = adam_update(
        decoder_weight, decoder_first, decoder_second, decoder_grad
    )
    return (
        encoder_next,
        encoder_first_next,
        encoder_second_next,
        decoder_next,
        decoder_first_next,
        decoder_second_next,
        encoder_bias_grad,
        decoder_bias_grad,
    )


def gathered_step(
    stream_rows,
    active_blocks,
    encoder_weight,
    encoder_bias,
    decoder_weight,
    decoder_bias,
    encoder_first,
    encoder_second,
    decoder_first,
    decoder_second,
):
    lat_count = lax.axis_size("lat")
    lat_here = lax.axis_index("lat")
    row_count, width_part = stream_rows.shape
    picks = active_blocks.shape[1]
    block = encoder_weight.shape[1]
    loss_scale = 1.0 / math.sqrt(picks * row_count)
    rows_all = lax.all_gather(stream_rows, "lat", axis=0, tiled=True)
    decoder_all = lax.all_gather(decoder_weight, "lat", axis=0, tiled=True)
    blocks_all = lax.all_gather(active_blocks, "lat", axis=0, tiled=True)
    live = jnp.any(blocks_all == lat_here, axis=1)[:, None]
    preact_part = jnp.dot(rows_all, encoder_weight, preferred_element_type=jnp.float32)
    preact = lax.psum(preact_part, "row") + encoder_bias
    code_vals = jnp.where(live, jax.nn.softplus(preact), 0.0).astype(jnp.bfloat16)
    codes_here = lax.all_to_all(
        code_vals.reshape(lat_count, row_count, block), "lat", split_axis=0, concat_axis=0, tiled=True
    )
    codes_here = codes_here.transpose(1, 0, 2).reshape(row_count, lat_count * block)
    rebuilt = (
        jnp.dot(codes_here, decoder_all, preferred_element_type=jnp.float32) + decoder_bias
    )
    residual = rebuilt - stream_rows.astype(jnp.float32)
    decoder_bias_grad = lax.psum(loss_scale * jnp.sum(residual, axis=0), "lat")
    error_local = (residual * loss_scale).astype(jnp.bfloat16)
    errors_all = lax.all_gather(error_local, "lat", axis=0, tiled=True)
    code_part = contract_cols(error_local, decoder_all)
    code_grad = lax.psum(code_part, "row").astype(jnp.bfloat16)
    code_grad = lax.all_to_all(
        code_grad.reshape(row_count, lat_count, block).transpose(1, 0, 2),
        "lat",
        split_axis=0,
        concat_axis=0,
        tiled=True,
    ).reshape(lat_count * row_count, block)
    preact_grad = jnp.where(live, code_grad.astype(jnp.float32) * jax.nn.sigmoid(preact), 0.0)
    encoder_bias_grad = jnp.sum(preact_grad, axis=0)
    preact_low = preact_grad.astype(jnp.bfloat16)
    encoder_grad = contract_rows(rows_all, preact_low)
    decoder_grad = contract_rows(code_vals, errors_all)
    encoder_next, encoder_first_next, encoder_second_next = adam_update(
        encoder_weight, encoder_first, encoder_second, encoder_grad
    )
    decoder_next, decoder_first_next, decoder_second_next = adam_update(
        decoder_weight, decoder_first, decoder_second, decoder_grad
    )
    return (
        encoder_next,
        encoder_first_next,
        encoder_second_next,
        decoder_next,
        decoder_first_next,
        decoder_second_next,
        encoder_bias_grad,
        decoder_bias_grad,
    )


def solution(mesh):
    return jax.shard_map(
        gathered_step if mesh.shape["lat"] <= 8 else routed_step,
        mesh=mesh,
        in_specs=(
            P(("groups", "lat"), "row"),
            P(("groups", "lat"), None),
            P(("groups", "row"), "lat"),
            P(("groups", "lat")),
            P(("groups", "lat"), "row"),
            P(("groups", "row")),
            P(("groups", "row"), "lat"),
            P(("groups", "row"), "lat"),
            P(("groups", "lat"), "row"),
            P(("groups", "lat"), "row"),
        ),
        out_specs=(
            P(("groups", "row"), "lat"),
            P(("groups", "row"), "lat"),
            P(("groups", "row"), "lat"),
            P(("groups", "lat"), "row"),
            P(("groups", "lat"), "row"),
            P(("groups", "lat"), "row"),
            P(("groups", "lat")),
            P(("groups", "row")),
        ),
        check_vma=False,
    )
```

```python
import functools
import math

import jax
import jax.numpy as jnp
from jax import lax
from jax.experimental import pallas as pl
from jax.experimental.pallas import tpu as pltpu
from jax.sharding import PartitionSpec as P

beta_one = 0.9
beta_two = 0.999
step_rate = 0.01
epsilon = 1e-08


def adam_update(weight, moment_one, moment_two, gradient):
    first_next = beta_one * moment_one.astype(jnp.float32) + (1.0 - beta_one) * gradient
    second_next = beta_two * moment_two.astype(jnp.float32) + (1.0 - beta_two) * gradient * gradient
    weight_next = weight.astype(jnp.float32) - step_rate * first_next / (
        jnp.sqrt(second_next) + epsilon
    )
    return (
        weight_next.astype(jnp.bfloat16),
        first_next.astype(jnp.bfloat16),
        second_next.astype(jnp.bfloat16),
    )


def contract_rows(left, right):
    return lax.dot_general(
        left, right, (((0,), (0,)), ((), ())), preferred_element_type=jnp.float32
    )


def contract_cols(left, right):
    return lax.dot_general(
        left, right, (((1,), (1,)), ((), ())), preferred_element_type=jnp.float32
    )


def routed_step(
    stream_rows,
    active_blocks,
    encoder_weight,
    encoder_bias,
    decoder_weight,
    decoder_bias,
    encoder_first,
    encoder_second,
    decoder_first,
    decoder_second,
):
    lat_count = lax.axis_size("lat")
    row_count = stream_rows.shape[0]
    width_part = stream_rows.shape[1]
    picks = active_blocks.shape[1]
    capacity = min(row_count, 2 * row_count * picks // lat_count)
    slot_total = lat_count * capacity
    loss_scale = 1.0 / math.sqrt(picks * row_count)
    chosen = active_blocks.reshape(-1)
    one_hot = (chosen[:, None] == jnp.arange(lat_count, dtype=jnp.int32)[None, :]).astype(jnp.int32)
    position = jnp.sum((jnp.cumsum(one_hot, axis=0) - 1) * one_hot, axis=1)
    slot_index = chosen * capacity + position
    owner_row = jnp.arange(chosen.shape[0], dtype=jnp.int32) // picks
    slot_row = jnp.zeros((slot_total,), jnp.int32).at[slot_index].set(owner_row)
    slot_live = jnp.zeros((slot_total,), jnp.bfloat16).at[slot_index].set(1.0)
    outgoing = (stream_rows[slot_row] * slot_live[:, None]).reshape(lat_count, capacity, width_part)
    routed_rows = lax.all_to_all(outgoing, "lat", split_axis=0, concat_axis=0, tiled=True).reshape(
        slot_total, width_part
    )
    preact_part = jnp.dot(routed_rows, encoder_weight, preferred_element_type=jnp.float32)
    preact = lax.psum(preact_part, "row") + encoder_bias
    code_vals = jax.nn.softplus(preact).astype(jnp.bfloat16)
    portion = jnp.dot(code_vals, decoder_weight, preferred_element_type=jnp.float32).astype(
        jnp.bfloat16
    )
    returned = lax.all_to_all(
        portion.reshape(lat_count, capacity, width_part),
        "lat",
        split_axis=0,
        concat_axis=0,
        tiled=True,
    )
    picked = returned.reshape(slot_total, width_part)[slot_index].reshape(
        row_count, picks, width_part
    )
    rebuilt = jnp.sum(picked.astype(jnp.float32), axis=1) + decoder_bias
    residual = rebuilt - stream_rows.astype(jnp.float32)
    decoder_bias_grad = lax.psum(loss_scale * jnp.sum(residual, axis=0), "lat")
    error_local = (residual * loss_scale).astype(jnp.bfloat16)
    outgoing_error = (error_local[slot_row] * slot_live[:, None]).reshape(
        lat_count, capacity, width_part
    )
    routed_error = lax.all_to_all(
        outgoing_error, "lat", split_axis=0, concat_axis=0, tiled=True
    ).reshape(slot_total, width_part)
    code_part = contract_cols(routed_error, decoder_weight)
    code_grad = lax.psum(code_part, "row")
    preact_grad = code_grad * jax.nn.sigmoid(preact)
    encoder_bias_grad = jnp.sum(preact_grad, axis=0)
    preact_low = preact_grad.astype(jnp.bfloat16)
    encoder_grad = contract_rows(routed_rows, preact_low)
    decoder_grad = contract_rows(code_vals, routed_error)
    encoder_next, encoder_first_next, encoder_second_next = adam_update(
        encoder_weight, encoder_first, encoder_second, encoder_grad
    )
    decoder_next, decoder_first_next, decoder_second_next = adam_update(
        decoder_weight, decoder_first, decoder_second, decoder_grad
    )
    return (
        encoder_next,
        encoder_first_next,
        encoder_second_next,
        decoder_next,
        decoder_first_next,
        decoder_second_next,
        encoder_bias_grad,
        decoder_bias_grad,
    )


PIECES = 2
TILE = 512


def step_kernel(
    lat_count,
    loss_scale,
    rows_ref,
    mask_ref,
    enc_ref,
    ebias_ref,
    dec_ref,
    dbias_ref,
    enc_grad_ref,
    dec_grad_ref,
    enc_bias_grad_ref,
    dec_bias_grad_ref,
    rows_all,
    dec_all,
    err_all,
    masks,
    part_mine,
    part_other,
    preact,
    code_mine,
    code_here,
    grad_mine,
    grad_other,
    grad_out,
    grad_in,
    sums,
    gather_send,
    gather_recv,
    small_send,
    small_recv,
):
    count, width = rows_ref.shape
    chips = lat_count // 2
    me = lax.axis_index("lat")
    other = 1 - lax.axis_index("row")
    chip, core = me // 2, me % 2
    mate = chip * 2 + 1 - core
    piece = count // PIECES
    mesh_id = pl.DeviceIdType.MESH
    buffers = (rows_all, dec_all, err_all)

    barrier = pltpu.get_barrier_semaphore()
    for step in range(1, lat_count):
        pl.semaphore_signal(
            barrier, inc=1, device_id={"lat": (me + step) % lat_count}, device_id_type=mesh_id
        )
    pl.semaphore_signal(barrier, inc=1, device_id={"row": other}, device_id_type=mesh_id)
    pl.semaphore_wait(barrier, lat_count)

    def span(at):
        return pl.ds(pl.multiple_of(at * count, count), count)

    def gather_copy(which, way, owner, part, target):
        view = buffers[which].at[pl.ds(pl.multiple_of(owner * count + part * piece, piece), piece)]
        return pltpu.make_async_remote_copy(
            src_ref=view,
            dst_ref=view,
            send_sem=gather_send.at[which, way, owner, part],
            recv_sem=gather_recv.at[which, owner, part],
            device_id={"lat": target},
            device_id_type=mesh_id,
        )

    def each_way(which, owner, part, way, act):
        if way == 0:
            pl.when(chip < chips - 1)(lambda: act(gather_copy(which, 0, owner, part, me + 2)))
        elif way == 1:
            pl.when(chip > 0)(lambda: act(gather_copy(which, 1, owner, part, me - 2)))
        else:
            act(gather_copy(which, 2, owner, part, mate))

    def begin(copy):
        copy.start()

    def sent(copy):
        copy.wait_send()

    def own_way(which, way):
        for part in range(PIECES):
            each_way(which, me, part, way, begin)

    def arrived(which, owner, part):
        gather_copy(which, 2, owner, part, mate).wait_recv()

    def pass_on(which, step, then=None):
        for part in range(PIECES):
            for way, owner, there in (
                (0, me - 2 * step, chip >= step),
                (1, me + 2 * step, chip + step < chips),
            ):
                @pl.when(there)
                def _():
                    arrived(which, owner, part)
                    each_way(which, owner, part, way, begin)
                    each_way(which, owner, part, 2, begin)
                    if then is not None and part == PIECES - 1:
                        then(owner)

    def from_mate(which, step, then=None):
        if step == 0:
            for part in range(PIECES):
                arrived(which, mate, part)
            if then is not None:
                then(mate)
            return
        for owner, there in ((mate - 2 * step, chip >= step), (mate + 2 * step, chip + step < chips)):
            @pl.when(there)
            def _():
                for part in range(PIECES):
                    arrived(which, owner, part)
                if then is not None:
                    then(owner)

    def all_sent(which):
        for part in range(PIECES):
            for way in range(3):
                each_way(which, me, part, way, sent)
        for step in range(1, chips):
            for part in range(PIECES):
                for way, owner, there in (
                    (0, me - 2 * step, chip >= step),
                    (1, me + 2 * step, chip + step < chips),
                ):
                    @pl.when(there)
                    def _():
                        each_way(which, owner, part, way, sent)
                        each_way(which, owner, part, 2, sent)

    def to_lat(kind, source, target_buffer, target):
        return pltpu.make_async_remote_copy(
            src_ref=source,
            dst_ref=target_buffer.at[me],
            send_sem=small_send.at[kind, target],
            recv_sem=small_recv.at[kind, me],
            device_id={"lat": target},
            device_id_type=mesh_id,
        )

    def from_lat(kind, target_buffer, source):
        return pltpu.make_async_remote_copy(
            src_ref=target_buffer.at[source],
            dst_ref=target_buffer.at[source],
            send_sem=small_send.at[kind, source],
            recv_sem=small_recv.at[kind, source],
            device_id={"lat": source},
            device_id_type=mesh_id,
        )

    def across(kind, mine, theirs, at):
        return pltpu.make_async_remote_copy(
            src_ref=mine.at[at],
            dst_ref=theirs.at[at],
            send_sem=small_send.at[kind, at],
            recv_sem=small_recv.at[kind, at],
            device_id={"row": other},
            device_id_type=mesh_id,
        )

    MASK, PART, CODE, GRAD, GRAD_OUT, SUM = range(6)

    rows_all[span(me)] = rows_ref[...]
    for way in range(3):
        own_way(0, way)
    for step in range(1, lat_count):
        target = (me + step) % lat_count
        to_lat(MASK, mask_ref.at[target], masks, target).start()
    masks[me] = mask_ref[me]
    dec_all[span(me)] = dec_ref[...]
    own_way(1, 2)

    def encode(owner):
        part_mine[owner] = jnp.dot(
            rows_all[span(owner)], enc_ref[...], preferred_element_type=jnp.float32
        )
        across(PART, part_mine, part_other, owner).start()

    encode(me)
    for step in range(chips):
        if step > 0:
            pass_on(0, step, encode)
            from_mate(0, step - 1, encode)
        pl.when(chip == step)(lambda: own_way(1, 0))
        pl.when(chip == chips - 1 - step)(lambda: own_way(1, 1))
    from_mate(0, chips - 1, encode)

    diagonal = lax.broadcasted_iota(jnp.int32, (count, count), 0) == lax.broadcasted_iota(
        jnp.int32, (count, count), 1
    )

    def live(owner):
        row = masks[owner][0:1, :].astype(jnp.float32)
        return jnp.sum(jnp.where(diagonal, row, 0.0), axis=1, keepdims=True)

    for owner in range(lat_count):
        @pl.when(owner != me)
        def _():
            from_lat(MASK, masks, owner).wait_recv()

        across(PART, part_mine, part_other, owner).wait_recv()
        value = part_mine[owner] + part_other[owner] + ebias_ref[...]
        preact[owner] = value
        soft = jnp.maximum(value, 0.0) + jnp.log1p(jnp.exp(-jnp.abs(value)))
        code_mine[owner] = (soft * live(owner)).astype(jnp.bfloat16)

        @pl.when(owner != me)
        def _():
            to_lat(CODE, code_mine.at[owner], code_here, owner).start()

        @pl.when(owner == me)
        def _():
            code_here[owner] = code_mine[owner]

    for step in range(1, chips):
        pass_on(1, step)
    for step in range(chips):
        from_mate(1, step)
    for owner in range(lat_count):
        @pl.when(owner != me)
        def _():
            from_lat(CODE, code_here, owner).wait_recv()

    codes = jnp.concatenate([code_here[at] for at in range(lat_count)], axis=1)
    for at in range(0, width, TILE):
        cols = slice(at, at + TILE)
        rebuilt = jnp.dot(codes, dec_all[:, cols], preferred_element_type=jnp.float32)
        residual = rebuilt + dbias_ref[:, cols] - rows_ref[:, cols].astype(jnp.float32)
        sums[me, :, cols] = loss_scale * jnp.sum(residual, axis=0, keepdims=True)
        err_all[span(me), cols] = (residual * loss_scale).astype(jnp.bfloat16)
    for way in range(3):
        own_way(2, way)
    errors = err_all[span(me)]
    for owner in range(lat_count):
        grad_mine[owner] = lax.dot_general(
            errors,
            dec_all[owner * count:(owner + 1) * count],
            (((1,), (1,)), ((), ())),
            preferred_element_type=jnp.float32,
        )
        across(GRAD, grad_mine, grad_other, owner).start()
    for step in range(1, lat_count):
        target = (me + step) % lat_count
        to_lat(SUM, sums.at[me], sums, target).start()
    for owner in range(lat_count):
        across(GRAD, grad_mine, grad_other, owner).wait_recv()
        grad_out[owner] = (grad_mine[owner] + grad_other[owner]).astype(jnp.bfloat16)

        @pl.when(owner != me)
        def _():
            to_lat(GRAD_OUT, grad_out.at[owner], grad_in, owner).start()

        @pl.when(owner == me)
        def _():
            grad_in[owner] = grad_out[owner]

    for step in range(1, chips - 1):
        pass_on(2, step)

    bias_total = jnp.zeros_like(enc_bias_grad_ref)
    lows = []
    for owner in range(lat_count):
        @pl.when(owner != me)
        def _():
            from_lat(GRAD_OUT, grad_in, owner).wait_recv()

        grad = grad_in[owner].astype(jnp.float32) * live(owner) * jax.nn.sigmoid(preact[owner])
        bias_total = bias_total + jnp.sum(grad, axis=0, keepdims=True)
        lows.append(grad.T.astype(jnp.bfloat16))
    enc_bias_grad_ref[...] = bias_total
    lows = jnp.concatenate(lows, axis=1)
    for at in range(0, width, TILE):
        cols = slice(at, at + TILE)
        enc_grad_ref[:, cols] = jnp.dot(lows, rows_all[:, cols], preferred_element_type=jnp.float32)
    for owner in range(lat_count):
        @pl.when(owner != me)
        def _():
            from_lat(SUM, sums, owner).wait_recv()
    total = sums[0]
    for owner in range(1, lat_count):
        total = total + sums[owner]
    dec_bias_grad_ref[...] = total
    turned = jnp.concatenate(
        [code_mine[at].astype(jnp.float32).T.astype(jnp.bfloat16) for at in range(lat_count)], axis=1
    )

    if chips > 1:
        pass_on(2, chips - 1)
    for step in range(chips):
        from_mate(2, step)
    for at in range(0, width, TILE):
        cols = slice(at, at + TILE)
        dec_grad_ref[:, cols] = jnp.dot(turned, err_all[:, cols], preferred_element_type=jnp.float32)

    for which in range(3):
        all_sent(which)
    for owner in range(lat_count):
        across(PART, part_mine, part_other, owner).wait_send()
        across(GRAD, grad_mine, grad_other, owner).wait_send()

        @pl.when(owner != me)
        def _():
            to_lat(MASK, mask_ref.at[owner], masks, owner).wait_send()
            to_lat(CODE, code_mine.at[owner], code_here, owner).wait_send()
            to_lat(GRAD_OUT, grad_out.at[owner], grad_in, owner).wait_send()
            to_lat(SUM, sums.at[me], sums, owner).wait_send()


def gathered_step(
    stream_rows,
    active_blocks,
    encoder_weight,
    encoder_bias,
    decoder_weight,
    decoder_bias,
    encoder_first,
    encoder_second,
    decoder_first,
    decoder_second,
):
    lat_count = lax.axis_size("lat")
    row_count, width = stream_rows.shape
    picks = active_blocks.shape[1]
    block = encoder_weight.shape[1]
    loss_scale = 1.0 / math.sqrt(picks * row_count)
    named = jnp.any(
        active_blocks[None, :, :] == jnp.arange(lat_count, dtype=jnp.int32)[:, None, None], axis=2
    )
    mask = jnp.broadcast_to(named[:, None, :], (lat_count, 16, row_count)).astype(jnp.bfloat16)
    low, full = jnp.bfloat16, jnp.float32
    everything = lat_count * row_count
    blocks = (lat_count, row_count, block)
    encoder_grad, decoder_grad, encoder_bias_grad, decoder_bias_grad = pl.pallas_call(
        functools.partial(step_kernel, lat_count, loss_scale),
        out_shape=(
            jax.ShapeDtypeStruct((block, width), full),
            jax.ShapeDtypeStruct((block, width), full),
            jax.ShapeDtypeStruct((1, block), full),
            jax.ShapeDtypeStruct((1, width), full),
        ),
        in_specs=[pl.BlockSpec(memory_space=pltpu.VMEM)] * 6,
        out_specs=[pl.BlockSpec(memory_space=pltpu.VMEM)] * 4,
        scratch_shapes=[
            pltpu.VMEM((everything, width), low),
            pltpu.VMEM((everything, width), low),
            pltpu.VMEM((everything, width), low),
            pltpu.VMEM((lat_count, 16, row_count), low),
            pltpu.VMEM(blocks, full),
            pltpu.VMEM(blocks, full),
            pltpu.VMEM(blocks, full),
            pltpu.VMEM(blocks, low),
            pltpu.VMEM(blocks, low),
            pltpu.VMEM(blocks, full),
            pltpu.VMEM(blocks, full),
            pltpu.VMEM(blocks, low),
            pltpu.VMEM(blocks, low),
            pltpu.VMEM((lat_count, 1, width), full),
            pltpu.SemaphoreType.DMA((3, 3, lat_count, PIECES)),
            pltpu.SemaphoreType.DMA((3, lat_count, PIECES)),
            pltpu.SemaphoreType.DMA((6, lat_count)),
            pltpu.SemaphoreType.DMA((6, lat_count)),
        ],
        compiler_params=pltpu.CompilerParams(
            collective_id=0, has_side_effects=True, vmem_limit_bytes=48 * 1024 * 1024
        ),
    )(
        stream_rows,
        mask,
        encoder_weight,
        encoder_bias.reshape(1, block),
        decoder_weight,
        decoder_bias.reshape(1, width),
    )
    encoder_next, encoder_first_next, encoder_second_next = adam_update(
        encoder_weight, encoder_first, encoder_second, encoder_grad.T
    )
    decoder_next, decoder_first_next, decoder_second_next = adam_update(
        decoder_weight, decoder_first, decoder_second, decoder_grad
    )
    return (
        encoder_next,
        encoder_first_next,
        encoder_second_next,
        decoder_next,
        decoder_first_next,
        decoder_second_next,
        encoder_bias_grad.reshape(-1),
        decoder_bias_grad.reshape(-1),
    )


def solution(mesh):
    return jax.shard_map(
        gathered_step if mesh.shape["lat"] <= 8 and mesh.shape["row"] == 2 else routed_step,
        mesh=mesh,
        in_specs=(
            P(("groups", "lat"), "row"),
            P(("groups", "lat"), None),
            P(("groups", "row"), "lat"),
            P(("groups", "lat")),
            P(("groups", "lat"), "row"),
            P(("groups", "row")),
            P(("groups", "row"), "lat"),
            P(("groups", "row"), "lat"),
            P(("groups", "lat"), "row"),
            P(("groups", "lat"), "row"),
        ),
        out_specs=(
            P(("groups", "row"), "lat"),
            P(("groups", "row"), "lat"),
            P(("groups", "row"), "lat"),
            P(("groups", "lat"), "row"),
            P(("groups", "lat"), "row"),
            P(("groups", "lat"), "row"),
            P(("groups", "lat")),
            P(("groups", "row")),
        ),
        check_vma=False,
    )
```

```python
import functools
import math

import jax
import jax.numpy as jnp
from jax import lax
from jax.experimental import pallas as pl
from jax.experimental.pallas import tpu as pltpu
from jax.sharding import PartitionSpec as P

beta_one = 0.9
beta_two = 0.999
step_rate = 0.01
epsilon = 1e-08


def adam_update(weight, moment_one, moment_two, gradient):
    first_next = beta_one * moment_one.astype(jnp.float32) + (1.0 - beta_one) * gradient
    second_next = beta_two * moment_two.astype(jnp.float32) + (1.0 - beta_two) * gradient * gradient
    weight_next = weight.astype(jnp.float32) - step_rate * first_next / (
        jnp.sqrt(second_next) + epsilon
    )
    return (
        weight_next.astype(jnp.bfloat16),
        first_next.astype(jnp.bfloat16),
        second_next.astype(jnp.bfloat16),
    )


def contract_rows(left, right):
    return lax.dot_general(
        left, right, (((0,), (0,)), ((), ())), preferred_element_type=jnp.float32
    )


def contract_cols(left, right):
    return lax.dot_general(
        left, right, (((1,), (1,)), ((), ())), preferred_element_type=jnp.float32
    )


def routed_step(
    stream_rows,
    active_blocks,
    encoder_weight,
    encoder_bias,
    decoder_weight,
    decoder_bias,
    encoder_first,
    encoder_second,
    decoder_first,
    decoder_second,
):
    lat_count = lax.axis_size("lat")
    row_count = stream_rows.shape[0]
    width_part = stream_rows.shape[1]
    picks = active_blocks.shape[1]
    capacity = min(row_count, 2 * row_count * picks // lat_count)
    slot_total = lat_count * capacity
    loss_scale = 1.0 / math.sqrt(picks * row_count)
    chosen = active_blocks.reshape(-1)
    one_hot = (chosen[:, None] == jnp.arange(lat_count, dtype=jnp.int32)[None, :]).astype(jnp.int32)
    position = jnp.sum((jnp.cumsum(one_hot, axis=0) - 1) * one_hot, axis=1)
    slot_index = chosen * capacity + position
    owner_row = jnp.arange(chosen.shape[0], dtype=jnp.int32) // picks
    slot_row = jnp.zeros((slot_total,), jnp.int32).at[slot_index].set(owner_row)
    slot_live = jnp.zeros((slot_total,), jnp.bfloat16).at[slot_index].set(1.0)
    outgoing = (stream_rows[slot_row] * slot_live[:, None]).reshape(lat_count, capacity, width_part)
    routed_rows = lax.all_to_all(outgoing, "lat", split_axis=0, concat_axis=0, tiled=True).reshape(
        slot_total, width_part
    )
    preact_part = jnp.dot(routed_rows, encoder_weight, preferred_element_type=jnp.float32)
    preact = lax.psum(preact_part, "row") + encoder_bias
    code_vals = jax.nn.softplus(preact).astype(jnp.bfloat16)
    portion = jnp.dot(code_vals, decoder_weight, preferred_element_type=jnp.float32).astype(
        jnp.bfloat16
    )
    returned = lax.all_to_all(
        portion.reshape(lat_count, capacity, width_part),
        "lat",
        split_axis=0,
        concat_axis=0,
        tiled=True,
    )
    picked = returned.reshape(slot_total, width_part)[slot_index].reshape(
        row_count, picks, width_part
    )
    rebuilt = jnp.sum(picked.astype(jnp.float32), axis=1) + decoder_bias
    residual = rebuilt - stream_rows.astype(jnp.float32)
    decoder_bias_grad = lax.psum(loss_scale * jnp.sum(residual, axis=0), "lat")
    error_local = (residual * loss_scale).astype(jnp.bfloat16)
    outgoing_error = (error_local[slot_row] * slot_live[:, None]).reshape(
        lat_count, capacity, width_part
    )
    routed_error = lax.all_to_all(
        outgoing_error, "lat", split_axis=0, concat_axis=0, tiled=True
    ).reshape(slot_total, width_part)
    code_part = contract_cols(routed_error, decoder_weight)
    code_grad = lax.psum(code_part, "row")
    preact_grad = code_grad * jax.nn.sigmoid(preact)
    encoder_bias_grad = jnp.sum(preact_grad, axis=0)
    preact_low = preact_grad.astype(jnp.bfloat16)
    encoder_grad = contract_rows(routed_rows, preact_low)
    decoder_grad = contract_rows(code_vals, routed_error)
    encoder_next, encoder_first_next, encoder_second_next = adam_update(
        encoder_weight, encoder_first, encoder_second, encoder_grad
    )
    decoder_next, decoder_first_next, decoder_second_next = adam_update(
        decoder_weight, decoder_first, decoder_second, decoder_grad
    )
    return (
        encoder_next,
        encoder_first_next,
        encoder_second_next,
        decoder_next,
        decoder_first_next,
        decoder_second_next,
        encoder_bias_grad,
        decoder_bias_grad,
    )


PIECES = 2
TILE = 512


def step_kernel(
    lat_count,
    loss_scale,
    rows_ref,
    mask_ref,
    enc_ref,
    ebias_ref,
    dec_ref,
    dbias_ref,
    enc_grad_ref,
    dec_grad_ref,
    enc_bias_grad_ref,
    dec_bias_grad_ref,
    rows_all,
    dec_all,
    err_all,
    masks,
    part_mine,
    part_other,
    preact,
    code_mine,
    code_here,
    grad_mine,
    grad_other,
    grad_out,
    grad_in,
    sums,
    gather_send,
    gather_recv,
    small_send,
    small_recv,
):
    count, width = rows_ref.shape
    chips = lat_count // 2
    me = lax.axis_index("lat")
    other = 1 - lax.axis_index("row")
    chip, core = me // 2, me % 2
    mate = chip * 2 + 1 - core
    piece = count // PIECES
    mesh_id = pl.DeviceIdType.MESH
    buffers = (rows_all, dec_all, err_all)

    barrier = pltpu.get_barrier_semaphore()
    for step in range(1, lat_count):
        pl.semaphore_signal(
            barrier, inc=1, device_id={"lat": (me + step) % lat_count}, device_id_type=mesh_id
        )
    pl.semaphore_signal(barrier, inc=1, device_id={"row": other}, device_id_type=mesh_id)
    pl.semaphore_wait(barrier, lat_count)

    def span(at):
        return pl.ds(pl.multiple_of(at * count, count), count)

    def gather_copy(which, way, owner, part, target):
        view = buffers[which].at[pl.ds(pl.multiple_of(owner * count + part * piece, piece), piece)]
        return pltpu.make_async_remote_copy(
            src_ref=view,
            dst_ref=view,
            send_sem=gather_send.at[which, way, owner, part],
            recv_sem=gather_recv.at[which, owner, part],
            device_id={"lat": target},
            device_id_type=mesh_id,
        )

    def each_way(which, owner, part, way, act):
        if way == 0:
            pl.when(chip < chips - 1)(lambda: act(gather_copy(which, 0, owner, part, me + 2)))
        elif way == 1:
            pl.when(chip > 0)(lambda: act(gather_copy(which, 1, owner, part, me - 2)))
        else:
            act(gather_copy(which, 2, owner, part, mate))

    def begin(copy):
        copy.start()

    def sent(copy):
        copy.wait_send()

    def own_way(which, way):
        for part in range(PIECES):
            each_way(which, me, part, way, begin)

    def arrived(which, owner, part):
        gather_copy(which, 2, owner, part, mate).wait_recv()

    def pass_on(which, step, then=None):
        for part in range(PIECES):
            for way, owner, there in (
                (0, me - 2 * step, chip >= step),
                (1, me + 2 * step, chip + step < chips),
            ):
                @pl.when(there)
                def _():
                    arrived(which, owner, part)
                    each_way(which, owner, part, way, begin)
                    each_way(which, owner, part, 2, begin)
                    if then is not None and part == PIECES - 1:
                        then(owner)

    def from_mate(which, step, then=None):
        if step == 0:
            for part in range(PIECES):
                arrived(which, mate, part)
            if then is not None:
                then(mate)
            return
        for owner, there in ((mate - 2 * step, chip >= step), (mate + 2 * step, chip + step < chips)):
            @pl.when(there)
            def _():
                for part in range(PIECES):
                    arrived(which, owner, part)
                if then is not None:
                    then(owner)

    def all_sent(which):
        for part in range(PIECES):
            for way in range(3):
                each_way(which, me, part, way, sent)
        for step in range(1, chips):
            for part in range(PIECES):
                for way, owner, there in (
                    (0, me - 2 * step, chip >= step),
                    (1, me + 2 * step, chip + step < chips),
                ):
                    @pl.when(there)
                    def _():
                        each_way(which, owner, part, way, sent)
                        each_way(which, owner, part, 2, sent)

    def to_lat(kind, source, target_buffer, target):
        return pltpu.make_async_remote_copy(
            src_ref=source,
            dst_ref=target_buffer.at[me],
            send_sem=small_send.at[kind, target],
            recv_sem=small_recv.at[kind, me],
            device_id={"lat": target},
            device_id_type=mesh_id,
        )

    def from_lat(kind, target_buffer, source):
        return pltpu.make_async_remote_copy(
            src_ref=target_buffer.at[source],
            dst_ref=target_buffer.at[source],
            send_sem=small_send.at[kind, source],
            recv_sem=small_recv.at[kind, source],
            device_id={"lat": source},
            device_id_type=mesh_id,
        )

    def across(kind, mine, theirs, at):
        return pltpu.make_async_remote_copy(
            src_ref=mine.at[at],
            dst_ref=theirs.at[at],
            send_sem=small_send.at[kind, at],
            recv_sem=small_recv.at[kind, at],
            device_id={"row": other},
            device_id_type=mesh_id,
        )

    MASK, PART, CODE, GRAD, GRAD_OUT, SUM = range(6)

    rows_all[span(me)] = rows_ref[...]
    for way in range(3):
        own_way(0, way)
    for step in range(1, lat_count):
        target = (me + step) % lat_count
        to_lat(MASK, mask_ref.at[target], masks, target).start()
    masks[me] = mask_ref[me]
    dec_all[span(me)] = dec_ref[...]
    own_way(1, 2)

    def encode(owner):
        part_mine[owner] = jnp.dot(
            rows_all[span(owner)], enc_ref[...], preferred_element_type=jnp.float32
        )
        across(PART, part_mine, part_other, owner).start()

    encode(me)
    for step in range(chips):
        if step > 0:
            pass_on(0, step, encode)
            from_mate(0, step - 1, encode)
        pl.when(chip == step)(lambda: own_way(1, 0))
        pl.when(chip == chips - 1 - step)(lambda: own_way(1, 1))
    from_mate(0, chips - 1, encode)

    diagonal = lax.broadcasted_iota(jnp.int32, (count, count), 0) == lax.broadcasted_iota(
        jnp.int32, (count, count), 1
    )

    def live(owner):
        row = masks[owner][0:1, :].astype(jnp.float32)
        return jnp.sum(jnp.where(diagonal, row, 0.0), axis=1, keepdims=True)

    for owner in range(lat_count):
        @pl.when(owner != me)
        def _():
            from_lat(MASK, masks, owner).wait_recv()

        across(PART, part_mine, part_other, owner).wait_recv()
        value = part_mine[owner] + part_other[owner] + ebias_ref[...]
        preact[owner] = value
        soft = jnp.maximum(value, 0.0) + jnp.log1p(jnp.exp(-jnp.abs(value)))
        code_mine[owner] = (soft * live(owner)).astype(jnp.bfloat16)

        @pl.when(owner != me)
        def _():
            to_lat(CODE, code_mine.at[owner], code_here, owner).start()

        @pl.when(owner == me)
        def _():
            code_here[owner] = code_mine[owner]

    for step in range(1, chips):
        pass_on(1, step)
    for step in range(chips):
        from_mate(1, step)
    for owner in range(lat_count):
        @pl.when(owner != me)
        def _():
            from_lat(CODE, code_here, owner).wait_recv()

    codes = jnp.concatenate([code_here[at] for at in range(lat_count)], axis=1)
    for at in range(0, width, TILE):
        cols = slice(at, at + TILE)
        rebuilt = jnp.dot(codes, dec_all[:, cols], preferred_element_type=jnp.float32)
        residual = rebuilt + dbias_ref[:, cols] - rows_ref[:, cols].astype(jnp.float32)
        sums[me, :, cols] = loss_scale * jnp.sum(residual, axis=0, keepdims=True)
        err_all[span(me), cols] = (residual * loss_scale).astype(jnp.bfloat16)
    for way in range(3):
        own_way(2, way)
    errors = err_all[span(me)]
    for owner in range(lat_count):
        grad_mine[owner] = lax.dot_general(
            errors,
            dec_all[owner * count:(owner + 1) * count],
            (((1,), (1,)), ((), ())),
            preferred_element_type=jnp.float32,
        )
        across(GRAD, grad_mine, grad_other, owner).start()
    for step in range(1, lat_count):
        target = (me + step) % lat_count
        to_lat(SUM, sums.at[me], sums, target).start()
    for owner in range(lat_count):
        across(GRAD, grad_mine, grad_other, owner).wait_recv()
        grad_out[owner] = (grad_mine[owner] + grad_other[owner]).astype(jnp.bfloat16)

        @pl.when(owner != me)
        def _():
            to_lat(GRAD_OUT, grad_out.at[owner], grad_in, owner).start()

        @pl.when(owner == me)
        def _():
            grad_in[owner] = grad_out[owner]

    for step in range(1, chips - 1):
        pass_on(2, step)

    bias_total = jnp.zeros_like(enc_bias_grad_ref)
    lows = []
    for owner in range(lat_count):
        @pl.when(owner != me)
        def _():
            from_lat(GRAD_OUT, grad_in, owner).wait_recv()

        grad = grad_in[owner].astype(jnp.float32) * live(owner) * jax.nn.sigmoid(preact[owner])
        bias_total = bias_total + jnp.sum(grad, axis=0, keepdims=True)
        lows.append(grad.T.astype(jnp.bfloat16))
    enc_bias_grad_ref[...] = bias_total
    lows = jnp.concatenate(lows, axis=1)
    for at in range(0, width, TILE):
        cols = slice(at, at + TILE)
        enc_grad_ref[cols, :] = jnp.dot(
            lows, rows_all[:, cols], preferred_element_type=jnp.float32
        ).T
    for owner in range(lat_count):
        @pl.when(owner != me)
        def _():
            from_lat(SUM, sums, owner).wait_recv()
    total = sums[0]
    for owner in range(1, lat_count):
        total = total + sums[owner]
    dec_bias_grad_ref[...] = total
    turned = jnp.concatenate(
        [code_mine[at].astype(jnp.float32).T.astype(jnp.bfloat16) for at in range(lat_count)], axis=1
    )

    if chips > 1:
        pass_on(2, chips - 1)
    for step in range(chips):
        from_mate(2, step)
    for at in range(0, width, TILE):
        cols = slice(at, at + TILE)
        dec_grad_ref[:, cols] = jnp.dot(turned, err_all[:, cols], preferred_element_type=jnp.float32)

    for which in range(3):
        all_sent(which)
    for owner in range(lat_count):
        across(PART, part_mine, part_other, owner).wait_send()
        across(GRAD, grad_mine, grad_other, owner).wait_send()

        @pl.when(owner != me)
        def _():
            to_lat(MASK, mask_ref.at[owner], masks, owner).wait_send()
            to_lat(CODE, code_mine.at[owner], code_here, owner).wait_send()
            to_lat(GRAD_OUT, grad_out.at[owner], grad_in, owner).wait_send()
            to_lat(SUM, sums.at[me], sums, owner).wait_send()


def gathered_step(
    stream_rows,
    active_blocks,
    encoder_weight,
    encoder_bias,
    decoder_weight,
    decoder_bias,
    encoder_first,
    encoder_second,
    decoder_first,
    decoder_second,
):
    lat_count = lax.axis_size("lat")
    row_count, width = stream_rows.shape
    picks = active_blocks.shape[1]
    block = encoder_weight.shape[1]
    loss_scale = 1.0 / math.sqrt(picks * row_count)
    named = jnp.any(
        active_blocks[None, :, :] == jnp.arange(lat_count, dtype=jnp.int32)[:, None, None], axis=2
    )
    mask = jnp.broadcast_to(named[:, None, :], (lat_count, 16, row_count)).astype(jnp.bfloat16)
    low, full = jnp.bfloat16, jnp.float32
    everything = lat_count * row_count
    blocks = (lat_count, row_count, block)
    encoder_grad, decoder_grad, encoder_bias_grad, decoder_bias_grad = pl.pallas_call(
        functools.partial(step_kernel, lat_count, loss_scale),
        out_shape=(
            jax.ShapeDtypeStruct((width, block), full),
            jax.ShapeDtypeStruct((block, width), full),
            jax.ShapeDtypeStruct((1, block), full),
            jax.ShapeDtypeStruct((1, width), full),
        ),
        in_specs=[pl.BlockSpec(memory_space=pltpu.VMEM)] * 6,
        out_specs=[pl.BlockSpec(memory_space=pltpu.VMEM)] * 4,
        scratch_shapes=[
            pltpu.VMEM((everything, width), low),
            pltpu.VMEM((everything, width), low),
            pltpu.VMEM((everything, width), low),
            pltpu.VMEM((lat_count, 16, row_count), low),
            pltpu.VMEM(blocks, full),
            pltpu.VMEM(blocks, full),
            pltpu.VMEM(blocks, full),
            pltpu.VMEM(blocks, low),
            pltpu.VMEM(blocks, low),
            pltpu.VMEM(blocks, full),
            pltpu.VMEM(blocks, full),
            pltpu.VMEM(blocks, low),
            pltpu.VMEM(blocks, low),
            pltpu.VMEM((lat_count, 1, width), full),
            pltpu.SemaphoreType.DMA((3, 3, lat_count, PIECES)),
            pltpu.SemaphoreType.DMA((3, lat_count, PIECES)),
            pltpu.SemaphoreType.DMA((6, lat_count)),
            pltpu.SemaphoreType.DMA((6, lat_count)),
        ],
        compiler_params=pltpu.CompilerParams(
            collective_id=0, has_side_effects=True, vmem_limit_bytes=48 * 1024 * 1024
        ),
    )(
        stream_rows,
        mask,
        encoder_weight,
        encoder_bias.reshape(1, block),
        decoder_weight,
        decoder_bias.reshape(1, width),
    )
    encoder_next, encoder_first_next, encoder_second_next = adam_update(
        encoder_weight, encoder_first, encoder_second, encoder_grad
    )
    decoder_next, decoder_first_next, decoder_second_next = adam_update(
        decoder_weight, decoder_first, decoder_second, decoder_grad
    )
    return (
        encoder_next,
        encoder_first_next,
        encoder_second_next,
        decoder_next,
        decoder_first_next,
        decoder_second_next,
        encoder_bias_grad.reshape(-1),
        decoder_bias_grad.reshape(-1),
    )


def solution(mesh):
    return jax.shard_map(
        gathered_step if mesh.shape["lat"] <= 8 and mesh.shape["row"] == 2 else routed_step,
        mesh=mesh,
        in_specs=(
            P(("groups", "lat"), "row"),
            P(("groups", "lat"), None),
            P(("groups", "row"), "lat"),
            P(("groups", "lat")),
            P(("groups", "lat"), "row"),
            P(("groups", "row")),
            P(("groups", "row"), "lat"),
            P(("groups", "row"), "lat"),
            P(("groups", "lat"), "row"),
            P(("groups", "lat"), "row"),
        ),
        out_specs=(
            P(("groups", "row"), "lat"),
            P(("groups", "row"), "lat"),
            P(("groups", "row"), "lat"),
            P(("groups", "lat"), "row"),
            P(("groups", "lat"), "row"),
            P(("groups", "lat"), "row"),
            P(("groups", "lat")),
            P(("groups", "row")),
        ),
        check_vma=False,
    )
```

```python
import functools
import math

import jax
import jax.numpy as jnp
from jax import lax
from jax.experimental import pallas as pl
from jax.experimental.pallas import tpu as pltpu
from jax.sharding import PartitionSpec as P

beta_one = 0.9
beta_two = 0.999
step_rate = 0.01
epsilon = 1e-08


def adam_update(weight, moment_one, moment_two, gradient):
    first_next = beta_one * moment_one.astype(jnp.float32) + (1.0 - beta_one) * gradient
    second_next = beta_two * moment_two.astype(jnp.float32) + (1.0 - beta_two) * gradient * gradient
    weight_next = weight.astype(jnp.float32) - step_rate * first_next / (
        jnp.sqrt(second_next) + epsilon
    )
    return (
        weight_next.astype(jnp.bfloat16),
        first_next.astype(jnp.bfloat16),
        second_next.astype(jnp.bfloat16),
    )


def contract_rows(left, right):
    return lax.dot_general(
        left, right, (((0,), (0,)), ((), ())), preferred_element_type=jnp.float32
    )


def contract_cols(left, right):
    return lax.dot_general(
        left, right, (((1,), (1,)), ((), ())), preferred_element_type=jnp.float32
    )


def routed_step(
    stream_rows,
    active_blocks,
    encoder_weight,
    encoder_bias,
    decoder_weight,
    decoder_bias,
    encoder_first,
    encoder_second,
    decoder_first,
    decoder_second,
):
    lat_count = lax.axis_size("lat")
    row_count = stream_rows.shape[0]
    width_part = stream_rows.shape[1]
    picks = active_blocks.shape[1]
    capacity = min(row_count, 2 * row_count * picks // lat_count)
    slot_total = lat_count * capacity
    loss_scale = 1.0 / math.sqrt(picks * row_count)
    chosen = active_blocks.reshape(-1)
    one_hot = (chosen[:, None] == jnp.arange(lat_count, dtype=jnp.int32)[None, :]).astype(jnp.int32)
    position = jnp.sum((jnp.cumsum(one_hot, axis=0) - 1) * one_hot, axis=1)
    slot_index = chosen * capacity + position
    owner_row = jnp.arange(chosen.shape[0], dtype=jnp.int32) // picks
    slot_row = jnp.zeros((slot_total,), jnp.int32).at[slot_index].set(owner_row)
    slot_live = jnp.zeros((slot_total,), jnp.bfloat16).at[slot_index].set(1.0)
    outgoing = (stream_rows[slot_row] * slot_live[:, None]).reshape(lat_count, capacity, width_part)
    routed_rows = lax.all_to_all(outgoing, "lat", split_axis=0, concat_axis=0, tiled=True).reshape(
        slot_total, width_part
    )
    preact_part = jnp.dot(routed_rows, encoder_weight, preferred_element_type=jnp.float32)
    preact = lax.psum(preact_part, "row") + encoder_bias
    code_vals = jax.nn.softplus(preact).astype(jnp.bfloat16)
    portion = jnp.dot(code_vals, decoder_weight, preferred_element_type=jnp.float32).astype(
        jnp.bfloat16
    )
    returned = lax.all_to_all(
        portion.reshape(lat_count, capacity, width_part),
        "lat",
        split_axis=0,
        concat_axis=0,
        tiled=True,
    )
    picked = returned.reshape(slot_total, width_part)[slot_index].reshape(
        row_count, picks, width_part
    )
    rebuilt = jnp.sum(picked.astype(jnp.float32), axis=1) + decoder_bias
    residual = rebuilt - stream_rows.astype(jnp.float32)
    decoder_bias_grad = lax.psum(loss_scale * jnp.sum(residual, axis=0), "lat")
    error_local = (residual * loss_scale).astype(jnp.bfloat16)
    outgoing_error = (error_local[slot_row] * slot_live[:, None]).reshape(
        lat_count, capacity, width_part
    )
    routed_error = lax.all_to_all(
        outgoing_error, "lat", split_axis=0, concat_axis=0, tiled=True
    ).reshape(slot_total, width_part)
    code_part = contract_cols(routed_error, decoder_weight)
    code_grad = lax.psum(code_part, "row")
    preact_grad = code_grad * jax.nn.sigmoid(preact)
    encoder_bias_grad = jnp.sum(preact_grad, axis=0)
    preact_low = preact_grad.astype(jnp.bfloat16)
    encoder_grad = contract_rows(routed_rows, preact_low)
    decoder_grad = contract_rows(code_vals, routed_error)
    encoder_next, encoder_first_next, encoder_second_next = adam_update(
        encoder_weight, encoder_first, encoder_second, encoder_grad
    )
    decoder_next, decoder_first_next, decoder_second_next = adam_update(
        decoder_weight, decoder_first, decoder_second, decoder_grad
    )
    return (
        encoder_next,
        encoder_first_next,
        encoder_second_next,
        decoder_next,
        decoder_first_next,
        decoder_second_next,
        encoder_bias_grad,
        decoder_bias_grad,
    )


PIECES = 2
TILE = 512


def step_kernel(
    lat_count,
    loss_scale,
    rows_ref,
    mask_ref,
    enc_ref,
    ebias_ref,
    dec_ref,
    dbias_ref,
    enc_grad_ref,
    dec_grad_ref,
    enc_bias_grad_ref,
    dec_bias_grad_ref,
    rows_all,
    dec_all,
    err_all,
    masks,
    part_mine,
    part_other,
    preact,
    code_mine,
    code_here,
    grad_mine,
    grad_other,
    grad_out,
    grad_in,
    sums,
    gather_send,
    gather_recv,
    small_send,
    small_recv,
    enc_here,
    load_sem,
):
    count, width = rows_ref.shape
    chips = lat_count // 2
    me = lax.axis_index("lat")
    other = 1 - lax.axis_index("row")
    chip, core = me // 2, me % 2
    mate = chip * 2 + 1 - core
    piece = count // PIECES
    mesh_id = pl.DeviceIdType.MESH
    buffers = (rows_all, dec_all, err_all)

    own = pl.ds(pl.multiple_of(me * count, count), count)
    load_rows = pltpu.make_async_copy(rows_ref, rows_all.at[own], load_sem.at[0])
    load_enc = pltpu.make_async_copy(enc_ref, enc_here, load_sem.at[1])
    load_dec = pltpu.make_async_copy(dec_ref, dec_all.at[own], load_sem.at[2])
    load_rows.start()
    load_enc.start()
    load_dec.start()
    barrier = pltpu.get_barrier_semaphore()
    for step in range(1, lat_count):
        pl.semaphore_signal(
            barrier, inc=1, device_id={"lat": (me + step) % lat_count}, device_id_type=mesh_id
        )
    pl.semaphore_signal(barrier, inc=1, device_id={"row": other}, device_id_type=mesh_id)
    pl.semaphore_wait(barrier, lat_count)

    def span(at):
        return pl.ds(pl.multiple_of(at * count, count), count)

    def gather_copy(which, way, owner, part, target):
        view = buffers[which].at[pl.ds(pl.multiple_of(owner * count + part * piece, piece), piece)]
        return pltpu.make_async_remote_copy(
            src_ref=view,
            dst_ref=view,
            send_sem=gather_send.at[which, way, owner, part],
            recv_sem=gather_recv.at[which, owner, part],
            device_id={"lat": target},
            device_id_type=mesh_id,
        )

    def each_way(which, owner, part, way, act):
        if way == 0:
            pl.when(chip < chips - 1)(lambda: act(gather_copy(which, 0, owner, part, me + 2)))
        elif way == 1:
            pl.when(chip > 0)(lambda: act(gather_copy(which, 1, owner, part, me - 2)))
        else:
            act(gather_copy(which, 2, owner, part, mate))

    def begin(copy):
        copy.start()

    def sent(copy):
        copy.wait_send()

    def own_way(which, way):
        for part in range(PIECES):
            each_way(which, me, part, way, begin)

    def arrived(which, owner, part):
        gather_copy(which, 2, owner, part, mate).wait_recv()

    def pass_on(which, step, then=None):
        for part in range(PIECES):
            for way, owner, there in (
                (0, me - 2 * step, chip >= step),
                (1, me + 2 * step, chip + step < chips),
            ):
                @pl.when(there)
                def _():
                    arrived(which, owner, part)
                    each_way(which, owner, part, way, begin)
                    each_way(which, owner, part, 2, begin)
                    if then is not None and part == PIECES - 1:
                        then(owner)

    def from_mate(which, step, then=None):
        if step == 0:
            for part in range(PIECES):
                arrived(which, mate, part)
            if then is not None:
                then(mate)
            return
        for owner, there in ((mate - 2 * step, chip >= step), (mate + 2 * step, chip + step < chips)):
            @pl.when(there)
            def _():
                for part in range(PIECES):
                    arrived(which, owner, part)
                if then is not None:
                    then(owner)

    def all_sent(which):
        for part in range(PIECES):
            for way in range(3):
                each_way(which, me, part, way, sent)
        for step in range(1, chips):
            for part in range(PIECES):
                for way, owner, there in (
                    (0, me - 2 * step, chip >= step),
                    (1, me + 2 * step, chip + step < chips),
                ):
                    @pl.when(there)
                    def _():
                        each_way(which, owner, part, way, sent)
                        each_way(which, owner, part, 2, sent)

    def to_lat(kind, source, target_buffer, target):
        return pltpu.make_async_remote_copy(
            src_ref=source,
            dst_ref=target_buffer.at[me],
            send_sem=small_send.at[kind, target],
            recv_sem=small_recv.at[kind, me],
            device_id={"lat": target},
            device_id_type=mesh_id,
        )

    def from_lat(kind, target_buffer, source):
        return pltpu.make_async_remote_copy(
            src_ref=target_buffer.at[source],
            dst_ref=target_buffer.at[source],
            send_sem=small_send.at[kind, source],
            recv_sem=small_recv.at[kind, source],
            device_id={"lat": source},
            device_id_type=mesh_id,
        )

    def across(kind, mine, theirs, at):
        return pltpu.make_async_remote_copy(
            src_ref=mine.at[at],
            dst_ref=theirs.at[at],
            send_sem=small_send.at[kind, at],
            recv_sem=small_recv.at[kind, at],
            device_id={"row": other},
            device_id_type=mesh_id,
        )

    MASK, PART, CODE, GRAD, GRAD_OUT, SUM = range(6)

    load_rows.wait()
    for way in range(3):
        own_way(0, way)
    for step in range(1, lat_count):
        target = (me + step) % lat_count
        to_lat(MASK, mask_ref.at[target], masks, target).start()
    masks[me] = mask_ref[me]
    load_enc.wait()
    load_dec.wait()
    own_way(1, 2)

    def encode(owner):
        part_mine[owner] = jnp.dot(
            rows_all[span(owner)], enc_here[...], preferred_element_type=jnp.float32
        )
        across(PART, part_mine, part_other, owner).start()

    encode(me)
    for step in range(chips):
        if step > 0:
            pass_on(0, step, encode)
            from_mate(0, step - 1, encode)
        pl.when(chip == step)(lambda: own_way(1, 0))
        pl.when(chip == chips - 1 - step)(lambda: own_way(1, 1))
    from_mate(0, chips - 1, encode)

    diagonal = lax.broadcasted_iota(jnp.int32, (count, count), 0) == lax.broadcasted_iota(
        jnp.int32, (count, count), 1
    )

    def live(owner):
        row = masks[owner][0:1, :].astype(jnp.float32)
        return jnp.sum(jnp.where(diagonal, row, 0.0), axis=1, keepdims=True)

    for owner in range(lat_count):
        @pl.when(owner != me)
        def _():
            from_lat(MASK, masks, owner).wait_recv()

        across(PART, part_mine, part_other, owner).wait_recv()
        value = part_mine[owner] + part_other[owner] + ebias_ref[...]
        preact[owner] = value
        soft = jnp.maximum(value, 0.0) + jnp.log1p(jnp.exp(-jnp.abs(value)))
        code_mine[owner] = (soft * live(owner)).astype(jnp.bfloat16)

        @pl.when(owner != me)
        def _():
            to_lat(CODE, code_mine.at[owner], code_here, owner).start()

        @pl.when(owner == me)
        def _():
            code_here[owner] = code_mine[owner]

    for step in range(1, chips):
        pass_on(1, step)
    for step in range(chips):
        from_mate(1, step)
    for owner in range(lat_count):
        @pl.when(owner != me)
        def _():
            from_lat(CODE, code_here, owner).wait_recv()

    codes = jnp.concatenate([code_here[at] for at in range(lat_count)], axis=1)
    for at in range(0, width, TILE):
        cols = slice(at, at + TILE)
        rebuilt = jnp.dot(codes, dec_all[:, cols], preferred_element_type=jnp.float32)
        residual = rebuilt + dbias_ref[:, cols] - rows_all[span(me), cols].astype(jnp.float32)
        sums[me, :, cols] = loss_scale * jnp.sum(residual, axis=0, keepdims=True)
        err_all[span(me), cols] = (residual * loss_scale).astype(jnp.bfloat16)
    for way in range(3):
        own_way(2, way)
    errors = err_all[span(me)]
    for owner in range(lat_count):
        grad_mine[owner] = lax.dot_general(
            errors,
            dec_all[owner * count:(owner + 1) * count],
            (((1,), (1,)), ((), ())),
            preferred_element_type=jnp.float32,
        )
        across(GRAD, grad_mine, grad_other, owner).start()
    for step in range(1, lat_count):
        target = (me + step) % lat_count
        to_lat(SUM, sums.at[me], sums, target).start()
    for owner in range(lat_count):
        across(GRAD, grad_mine, grad_other, owner).wait_recv()
        grad_out[owner] = (grad_mine[owner] + grad_other[owner]).astype(jnp.bfloat16)

        @pl.when(owner != me)
        def _():
            to_lat(GRAD_OUT, grad_out.at[owner], grad_in, owner).start()

        @pl.when(owner == me)
        def _():
            grad_in[owner] = grad_out[owner]

    for step in range(1, chips - 1):
        pass_on(2, step)

    bias_total = jnp.zeros_like(enc_bias_grad_ref)
    lows = []
    for owner in range(lat_count):
        @pl.when(owner != me)
        def _():
            from_lat(GRAD_OUT, grad_in, owner).wait_recv()

        grad = grad_in[owner].astype(jnp.float32) * live(owner) * jax.nn.sigmoid(preact[owner])
        bias_total = bias_total + jnp.sum(grad, axis=0, keepdims=True)
        lows.append(grad.T.astype(jnp.bfloat16))
    enc_bias_grad_ref[...] = bias_total
    lows = jnp.concatenate(lows, axis=1)
    for at in range(0, width, TILE):
        cols = slice(at, at + TILE)
        enc_grad_ref[cols, :] = jnp.dot(
            lows, rows_all[:, cols], preferred_element_type=jnp.float32
        ).T
    for owner in range(lat_count):
        @pl.when(owner != me)
        def _():
            from_lat(SUM, sums, owner).wait_recv()
    total = sums[0]
    for owner in range(1, lat_count):
        total = total + sums[owner]
    dec_bias_grad_ref[...] = total
    turned = jnp.concatenate(
        [code_mine[at].astype(jnp.float32).T.astype(jnp.bfloat16) for at in range(lat_count)], axis=1
    )

    if chips > 1:
        pass_on(2, chips - 1)
    for step in range(chips):
        from_mate(2, step)
    for at in range(0, width, TILE):
        cols = slice(at, at + TILE)
        dec_grad_ref[:, cols] = jnp.dot(turned, err_all[:, cols], preferred_element_type=jnp.float32)

    for which in range(3):
        all_sent(which)
    for owner in range(lat_count):
        across(PART, part_mine, part_other, owner).wait_send()
        across(GRAD, grad_mine, grad_other, owner).wait_send()

        @pl.when(owner != me)
        def _():
            to_lat(MASK, mask_ref.at[owner], masks, owner).wait_send()
            to_lat(CODE, code_mine.at[owner], code_here, owner).wait_send()
            to_lat(GRAD_OUT, grad_out.at[owner], grad_in, owner).wait_send()
            to_lat(SUM, sums.at[me], sums, owner).wait_send()


def gathered_step(
    stream_rows,
    active_blocks,
    encoder_weight,
    encoder_bias,
    decoder_weight,
    decoder_bias,
    encoder_first,
    encoder_second,
    decoder_first,
    decoder_second,
):
    lat_count = lax.axis_size("lat")
    row_count, width = stream_rows.shape
    picks = active_blocks.shape[1]
    block = encoder_weight.shape[1]
    loss_scale = 1.0 / math.sqrt(picks * row_count)
    named = jnp.any(
        active_blocks[None, :, :] == jnp.arange(lat_count, dtype=jnp.int32)[:, None, None], axis=2
    )
    mask = jnp.broadcast_to(named[:, None, :], (lat_count, 16, row_count)).astype(jnp.bfloat16)
    low, full = jnp.bfloat16, jnp.float32
    everything = lat_count * row_count
    blocks = (lat_count, row_count, block)
    encoder_grad, decoder_grad, encoder_bias_grad, decoder_bias_grad = pl.pallas_call(
        functools.partial(step_kernel, lat_count, loss_scale),
        out_shape=(
            jax.ShapeDtypeStruct((width, block), full),
            jax.ShapeDtypeStruct((block, width), full),
            jax.ShapeDtypeStruct((1, block), full),
            jax.ShapeDtypeStruct((1, width), full),
        ),
        in_specs=[
            pl.BlockSpec(memory_space=pltpu.VMEM if at in (1, 3, 5) else pl.ANY) for at in range(6)
        ],
        out_specs=[pl.BlockSpec(memory_space=pltpu.VMEM)] * 4,
        scratch_shapes=[
            pltpu.VMEM((everything, width), low),
            pltpu.VMEM((everything, width), low),
            pltpu.VMEM((everything, width), low),
            pltpu.VMEM((lat_count, 16, row_count), low),
            pltpu.VMEM(blocks, full),
            pltpu.VMEM(blocks, full),
            pltpu.VMEM(blocks, full),
            pltpu.VMEM(blocks, low),
            pltpu.VMEM(blocks, low),
            pltpu.VMEM(blocks, full),
            pltpu.VMEM(blocks, full),
            pltpu.VMEM(blocks, low),
            pltpu.VMEM(blocks, low),
            pltpu.VMEM((lat_count, 1, width), full),
            pltpu.SemaphoreType.DMA((3, 3, lat_count, PIECES)),
            pltpu.SemaphoreType.DMA((3, lat_count, PIECES)),
            pltpu.SemaphoreType.DMA((6, lat_count)),
            pltpu.SemaphoreType.DMA((6, lat_count)),
            pltpu.VMEM((width, block), low),
            pltpu.SemaphoreType.DMA((3,)),
        ],
        compiler_params=pltpu.CompilerParams(
            collective_id=0, has_side_effects=True, vmem_limit_bytes=59 * 1024 * 1024
        ),
    )(
        stream_rows,
        mask,
        encoder_weight,
        encoder_bias.reshape(1, block),
        decoder_weight,
        decoder_bias.reshape(1, width),
    )
    encoder_next, encoder_first_next, encoder_second_next = adam_update(
        encoder_weight, encoder_first, encoder_second, encoder_grad
    )
    decoder_next, decoder_first_next, decoder_second_next = adam_update(
        decoder_weight, decoder_first, decoder_second, decoder_grad
    )
    return (
        encoder_next,
        encoder_first_next,
        encoder_second_next,
        decoder_next,
        decoder_first_next,
        decoder_second_next,
        encoder_bias_grad.reshape(-1),
        decoder_bias_grad.reshape(-1),
    )


def solution(mesh):
    return jax.shard_map(
        gathered_step if mesh.shape["lat"] <= 8 and mesh.shape["row"] == 2 else routed_step,
        mesh=mesh,
        in_specs=(
            P(("groups", "lat"), "row"),
            P(("groups", "lat"), None),
            P(("groups", "row"), "lat"),
            P(("groups", "lat")),
            P(("groups", "lat"), "row"),
            P(("groups", "row")),
            P(("groups", "row"), "lat"),
            P(("groups", "row"), "lat"),
            P(("groups", "lat"), "row"),
            P(("groups", "lat"), "row"),
        ),
        out_specs=(
            P(("groups", "row"), "lat"),
            P(("groups", "row"), "lat"),
            P(("groups", "row"), "lat"),
            P(("groups", "lat"), "row"),
            P(("groups", "lat"), "row"),
            P(("groups", "lat"), "row"),
            P(("groups", "lat")),
            P(("groups", "row")),
        ),
        check_vma=False,
    )
```
